32 devices in a mesh: hst: 4 (over z), dev: 8 (over y, x, core).
Axes of the slice: x: 2, y: 2, z: 4, core: 2. Of those that a mesh axis runs over, the one named last changes fastest.
Arguments:
- features: bfloat16 [65536, 768], P(('hst', 'dev')), may hold values from -6 to 6
- cache_blocks: bfloat16 [4, 2048, 768], P('hst', 'dev'), may hold values from -6 to 6
- plan: int32 [4, 16], P('hst', 'dev'), may hold values from 0 to 15, as said below
- miss_ids: int32 [32, 4, 8, 64], P(('hst', 'dev')), may hold values from 0 to 2303, as said below
- miss_counts: int32 [32, 4, 8], P(('hst', 'dev')), may hold values from 16 to 64, as said below
- self_ids: int32 [26624], P(('hst', 'dev')), may hold values from 0 to 2047, as said below
- nbr_ids: int32 [26624, 15], P(('hst', 'dev')), may hold values from 0 to 2047, as said below
- hop_counts: int32 [26624], P(('hst', 'dev')), may hold values from 1 to 15, as said below
- seed_counts: int32 [1024], P(('hst', 'dev')), may hold values from 1 to 25, as said below
- w_self1: bfloat16 [768, 1024], replicated, may hold values from -0.21875 to 0.21875
- w_nbr1: bfloat16 [768, 1024], replicated, may hold values from -0.21875 to 0.21875
- w_self2: bfloat16 [1024, 1024], replicated, may hold values from -0.1875 to 0.1875
- w_nbr2: bfloat16 [1024, 1024], replicated, may hold values from -0.1875 to 0.1875
- cotangent: bfloat16 [1024, 1024], P(('hst', 'dev')), may hold values from -0.29882812 to 0.29882812
Outputs:
- embedding: bfloat16 [1024, 1024], P(('hst', 'dev'))
- new_cache: bfloat16 [4, 2048, 768], P('hst', 'dev')
- grad_self1: float32 [768, 1024], P(None, ('hst', 'dev'))
- grad_nbr1: float32 [768, 1024], P(None, ('hst', 'dev'))
- grad_self2: float32 [1024, 1024], P(None, ('hst', 'dev'))
- grad_nbr2: float32 [1024, 1024], P(None, ('hst', 'dev'))
The draws below stay inside these ranges and needn't reach their ends.
Inputs may be any that keep to these rules, and one draw needn't show every extreme that they name: Within each cache domain h, plan[h] is a permutation of the 16 block numbers. `miss_ids`: row numbers into the peer's served table; slots at or past the count are unused. `miss_counts`: in every draw some peer is asked for 64 rows by every device. `self_ids`: each names a used fetched slot p * 64 + c of the same device, c below that device's count for peer p. `nbr_ids`: each names a used fetched slot p * 64 + c of the same device, c below that device's count for peer p. `hop_counts`: the first node of every device has 15. `seed_counts`: the first seed of every device has 25.
All inputs are finite; a program needn't handle non-finite values.
Results may differ from the reference program's by a relative error of at most 0.0052.
Values may be sent and summed in bfloat16 or wider, within the bound.
A program may use at most 128 MiB of HBM per device.

```python
import jax
import jax.numpy as jnp
from jax import lax

F = 768
H = 1024
FAN1 = 25
FAN2 = 15
SEED_DEV = 32
ROWS_DEV = 2048
CSLOT = 2
BLOCK = 128
CAP = 64
T1 = 832
NODES = 65536
SEEDS = 1024
N_HST = 4
N_DEV = 8


def fill_counts(key):
    device_count = N_HST * N_DEV
    lowest = max(CAP // 4, 1)
    counts = jax.random.randint(jax.random.fold_in(key, 11), (device_count, device_count), lowest, CAP + 1, dtype=jnp.int32)
    hot_peer = jax.random.randint(jax.random.fold_in(key, 12), (), 0, device_count, dtype=jnp.int32)
    counts = counts.at[:, hot_peer].set(CAP)
    return counts


def frontier_refs(key):
    device_count = N_HST * N_DEV
    counts = fill_counts(key)
    peer_pick = jax.random.randint(jax.random.fold_in(key, 31), (device_count, T1, FAN2 + 1), 0, device_count, dtype=jnp.int32)
    raw_bits = jax.random.randint(jax.random.fold_in(key, 32), (device_count, T1, FAN2 + 1), 0, 1 << 20, dtype=jnp.int32)
    device_index = jnp.arange(device_count, dtype=jnp.int32)[:, None, None]
    limit = counts[device_index, peer_pick]
    return (peer_pick * CAP + raw_bits % limit).astype(jnp.int32)


def draw_miss_counts(key, part):
    return fill_counts(key).reshape(N_HST * N_DEV, N_HST, N_DEV)


def draw_miss_ids(key, part):
    shape = (N_HST * N_DEV, N_HST, N_DEV, CAP)
    coin = jax.random.randint(jax.random.fold_in(key, 13), shape, 0, 2, dtype=jnp.int32)
    cached = ROWS_DEV + jax.random.randint(jax.random.fold_in(key, 14), shape, 0, CSLOT * BLOCK, dtype=jnp.int32)
    stored = jax.random.randint(jax.random.fold_in(key, 15), shape, 0, ROWS_DEV, dtype=jnp.int32)
    return jnp.where(coin == 1, cached, stored).astype(jnp.int32)


def draw_self_ids(key, part):
    return frontier_refs(key)[:, :, 0].reshape(N_HST * N_DEV * T1)


def draw_nbr_ids(key, part):
    return frontier_refs(key)[:, :, 1:].reshape(N_HST * N_DEV * T1, FAN2)


def draw_hop_counts(key, part):
    counts = jax.random.randint(jax.random.fold_in(key, 41), (N_HST * N_DEV, T1), 1, FAN2 + 1, dtype=jnp.int32)
    return counts.at[:, 0].set(FAN2).reshape(N_HST * N_DEV * T1)


def draw_seed_counts(key, part):
    counts = jax.random.randint(jax.random.fold_in(key, 42), (N_HST * N_DEV, SEED_DEV), 1, FAN1 + 1, dtype=jnp.int32)
    return counts.at[:, 0].set(FAN1).reshape(N_HST * N_DEV * SEED_DEV)


def draw_plan(key, part):
    host_keys = jax.random.split(jax.random.fold_in(key, 21), N_HST)
    orders = jax.vmap(lambda host_key: jax.random.permutation(host_key, N_DEV * CSLOT))(host_keys)
    return orders.astype(jnp.int32)


def with_spikes(values, own_key, source, target, blocks, factor):
    owner, partner = [(jnp.arange(values.shape[axis_at]) // (values.shape[axis_at] // blocks)).reshape([-1 if axis == axis_at else 1 for axis in range(values.ndim)]) for axis_at in (source, target)]
    chosen = jax.random.permutation(own_key, blocks)[partner]
    strong = (owner == chosen) | (owner == (partner + blocks // 2) % blocks)
    return jnp.where(strong, factor * values, values)


def block_scale(own_key, shape, pieces, least, largest):
    def one(position, parts):
        heights = jax.random.uniform(jax.random.fold_in(jax.random.fold_in(own_key, 6), position), (parts,), jnp.float32, least / len(pieces), largest / len(pieces))
        return jnp.repeat(jnp.exp(heights), shape[position] // parts).reshape((-1,) + (1,) * (len(shape) - position - 1))

    factor_of = one(*pieces[0])
    for cut in pieces[1:]:
        factor_of = factor_of * one(*cut)
    return factor_of


def normal_values(stream_key, extent, width, bound, pieces=(), held_as=jnp.bfloat16):
    values = jax.random.normal(stream_key, extent, jnp.float32) * width
    if len(pieces) > 0:
        values = block_scale(stream_key, extent, pieces, -0.22, 0.18) * values
    return jnp.clip(values, min=-bound, max=bound).astype(held_as)


def gaussian_with(own_key, dims, scale, most, pieces, heavy, held_as=jnp.bfloat16):
    entries = scale * jax.random.normal(own_key, dims, jnp.float32)
    if pieces:
        entries = entries * block_scale(own_key, dims, pieces, -0.22, 0.18)
    return jnp.clip(with_spikes(entries, jax.random.fold_in(own_key, 3), *heavy), -most, most).astype(held_as)


def setup_inputs(seed: int = 0) -> dict:
    splits = jax.random.split(jax.random.key(seed), 15)
    return {
        "features": normal_values(splits[0], (NODES, F), 1.0, 6.0, ((0, 32),)),
        "cache_blocks": normal_values(splits[1], (N_HST, N_DEV * CSLOT * BLOCK, F), 1.0, 6.0, ((0, 4), (1, 8))),
        "plan": draw_plan(jax.random.fold_in(splits[14], 71), 0),
        "miss_ids": draw_miss_ids(jax.random.fold_in(splits[14], 71), 0),
        "miss_counts": draw_miss_counts(jax.random.fold_in(splits[14], 71), 0),
        "self_ids": draw_self_ids(jax.random.fold_in(splits[14], 71), 0),
        "nbr_ids": draw_nbr_ids(jax.random.fold_in(splits[14], 71), 0),
        "hop_counts": draw_hop_counts(jax.random.fold_in(splits[14], 71), 0),
        "seed_counts": draw_seed_counts(jax.random.fold_in(splits[14], 71), 0),
        "w_self1": normal_values(splits[9], (F, H), F ** -0.5, 0.21875),
        "w_nbr1": normal_values(splits[10], (F, H), F ** -0.5, 0.21875),
        "w_self2": normal_values(splits[11], (H, H), H ** -0.5, 0.1875),
        "w_nbr2": normal_values(splits[12], (H, H), H ** -0.5, 0.1875),
        "cotangent": gaussian_with(splits[13], (SEEDS, H), 0.05, 0.29882812, ((0, 32),), (0, 1, 32, 2.75)),
    }


def local_step(frontier, self_rows, nbr_rows, count_one, count_two, w_self1, w_nbr1, w_self2, w_nbr2, cot_rows):
    own_rows = frontier[self_rows]
    mask_one = (jnp.arange(FAN2, dtype=jnp.int32)[None, :] < count_one[:, None])
    summed_one = jnp.zeros((own_rows.shape[0], F), jnp.float32)
    for k in range(FAN2):
        picked = frontier[nbr_rows[:, k]].astype(jnp.float32)
        summed_one = summed_one + jnp.where(mask_one[:, k][:, None], picked, jnp.zeros_like(picked))
    mean_one = (summed_one / count_one[:, None].astype(jnp.float32)).astype(jnp.bfloat16)
    hidden_pre = jnp.dot(own_rows, w_self1, preferred_element_type=jnp.float32) + jnp.dot(mean_one, w_nbr1, preferred_element_type=jnp.float32)
    hidden_one = jax.nn.silu(hidden_pre).astype(jnp.bfloat16)
    seed_rows = hidden_one[:SEED_DEV]
    hop_rows = hidden_one[SEED_DEV:].reshape(SEED_DEV, FAN1, H)
    mask_two = (jnp.arange(FAN1, dtype=jnp.int32)[None, :] < count_two[:, None]).astype(jnp.float32)
    summed_two = jnp.einsum("skh,sk->sh", hop_rows.astype(jnp.float32), mask_two)
    mean_two = (summed_two / count_two[:, None].astype(jnp.float32)).astype(jnp.bfloat16)
    embedding = (jnp.dot(seed_rows, w_self2, preferred_element_type=jnp.float32) + jnp.dot(mean_two, w_nbr2, preferred_element_type=jnp.float32)).astype(jnp.bfloat16)
    grad_self2 = jnp.dot(seed_rows.T, cot_rows, preferred_element_type=jnp.float32)
    grad_nbr2 = jnp.dot(mean_two.T, cot_rows, preferred_element_type=jnp.float32)
    back_self = jnp.dot(cot_rows, w_self2.T, preferred_element_type=jnp.float32)
    back_mean = jnp.dot(cot_rows, w_nbr2.T, preferred_element_type=jnp.float32) / count_two[:, None].astype(jnp.float32)
    back_hop = back_mean[:, None, :] * mask_two[:, :, None]
    back_hidden = jnp.concatenate([back_self, back_hop.reshape(SEED_DEV * FAN1, H)], 0)
    gate_value = jax.nn.sigmoid(hidden_pre)
    back_pre = (back_hidden * gate_value * (1.0 + hidden_pre * (1.0 - gate_value))).astype(jnp.bfloat16)
    grad_self1 = jnp.dot(own_rows.T, back_pre, preferred_element_type=jnp.float32)
    grad_nbr1 = jnp.dot(mean_one.T, back_pre, preferred_element_type=jnp.float32)
    return embedding, (grad_self1, grad_nbr1, grad_self2, grad_nbr2)


def reference(features, cache_blocks, plan, miss_ids, miss_counts, self_ids, nbr_ids, hop_counts, seed_counts, w_self1, w_nbr1, w_self2, w_nbr2, cotangent):
    device_count = N_HST * N_DEV
    cache_rows = CSLOT * BLOCK
    blocks = cache_blocks.reshape(N_HST, N_DEV * CSLOT, BLOCK, F)
    moved_blocks = jax.vmap(lambda group, order: group[order])(blocks, plan)
    new_cache = moved_blocks.reshape(N_HST, N_DEV * cache_rows, F)
    full_table = jnp.concatenate([features, new_cache.reshape(device_count * cache_rows, F)], 0)
    peer_index = jnp.arange(device_count, dtype=jnp.int32)[:, None]
    slot_index = jnp.arange(CAP, dtype=jnp.int32)[None, :]
    home_rows = ROWS_DEV * device_count

    def one_device(totals, inputs):
        asked, counted, self_rows, nbr_rows, count_one, count_two, cot_rows = inputs
        global_row = jnp.where(asked < ROWS_DEV, peer_index * ROWS_DEV + asked, home_rows + peer_index * cache_rows + asked - ROWS_DEV).astype(jnp.int32)
        row_data = full_table[global_row]
        is_valid = slot_index < counted[:, None]
        row_data = jnp.where(is_valid[:, :, None], row_data, jnp.zeros_like(row_data))
        frontier = row_data.reshape(device_count * CAP, F)
        embedding, grads = local_step(frontier, self_rows, nbr_rows, count_one, count_two, w_self1, w_nbr1, w_self2, w_nbr2, cot_rows)
        totals = tuple(total + grad for total, grad in zip(totals, grads))
        return totals, embedding

    start_totals = (jnp.zeros((F, H), jnp.float32), jnp.zeros((F, H), jnp.float32), jnp.zeros((H, H), jnp.float32), jnp.zeros((H, H), jnp.float32))
    inputs = (
        miss_ids.reshape(device_count, device_count, CAP),
        miss_counts.reshape(device_count, device_count),
        self_ids.reshape(device_count, T1),
        nbr_ids.reshape(device_count, T1, FAN2),
        hop_counts.reshape(device_count, T1),
        seed_counts.reshape(device_count, SEED_DEV),
        cotangent.reshape(device_count, SEED_DEV, H),
    )
    totals, embedded = lax.scan(one_device, start_totals, inputs)
    embedding = embedded.reshape(device_count * SEED_DEV, H)
    return (embedding, new_cache, totals[0], totals[1], totals[2], totals[3])
```

```python
import jax
import jax.numpy as jnp
from jax import lax
from jax.sharding import PartitionSpec as P

CSLOT = 2
BOTH = ("hst", "dev")


def pick_matrix(ids, used, valid, dtype=jnp.bfloat16):
    slots = valid.shape[0]
    slot = lax.broadcasted_iota(jnp.int32, (slots, ids.shape[1]), 0)
    named = jnp.where(used, ids, -1)
    total = jnp.zeros(slot.shape, jnp.float32)
    for k in range(ids.shape[0]):
        total = total + jnp.where(named[k][None, :] == slot, 1.0, 0.0)
    return jnp.where(valid[:, None], total, 0.0).astype(dtype)


def contract(left, right, dim_left, dim_right):
    return lax.dot_general(
        left, right, (((dim_left,), (dim_right,)), ((), ())), preferred_element_type=jnp.float32
    )


def local(
    features,
    cache_blocks,
    plan,
    miss_ids,
    miss_counts,
    self_ids,
    nbr_ids,
    hop_counts,
    seed_counts,
    w_self1,
    w_nbr1,
    w_self2,
    w_nbr2,
    cotangent,
):
    bf16, f32 = jnp.bfloat16, jnp.float32
    home_rows, width_in = features.shape
    slot_count = miss_ids.shape[3]
    n_hst, n_dev = lax.axis_size("hst"), lax.axis_size("dev")
    device_count = n_hst * n_dev
    nodes, fan2 = nbr_ids.shape
    seeds = seed_counts.shape[0]
    fan1 = (nodes - seeds) // seeds
    hidden = w_self1.shape[1]
    part = hidden // device_count
    cache_rows = cache_blocks.shape[1]
    block = cache_rows // CSLOT

    everyones = lax.all_gather(cache_blocks[0], "dev", axis=0, tiled=True)
    requests = lax.all_to_all(
        miss_ids.reshape(device_count, slot_count), BOTH, split_axis=0, concat_axis=0, tiled=True
    ).reshape(-1)
    cot_parts = cotangent.reshape(seeds, n_hst, n_dev, part).transpose(2, 0, 1, 3)
    cot_cols = lax.all_to_all(
        cot_parts.reshape(n_dev, seeds, n_hst * part), "dev", split_axis=0, concat_axis=0, tiled=True
    ).reshape(n_dev * seeds, n_hst * part)

    from_home = features[jnp.minimum(requests, home_rows - 1)]
    blocks = everyones.reshape(-1, block, width_in)
    new_cache = jnp.concatenate(
        [lax.dynamic_index_in_dim(blocks, plan[0, j], 0, keepdims=False) for j in range(CSLOT)], 0
    )
    row = lax.broadcasted_iota(jnp.int32, (cache_rows, requests.shape[0]), 0)
    in_cache = ((requests - home_rows)[None, :] == row).astype(bf16)
    from_cache = contract(in_cache, new_cache, 0, 0).astype(bf16)
    row_data = jnp.where((requests < home_rows)[:, None], from_home, from_cache)
    fetched = lax.all_to_all(
        row_data.reshape(device_count, slot_count, width_in), BOTH, split_axis=0, concat_axis=0, tiled=True
    ).reshape(device_count * slot_count, width_in)

    valid = (
        lax.broadcasted_iota(jnp.int32, (device_count, slot_count), 1)
        < miss_counts.reshape(device_count)[:, None]
    ).reshape(-1)
    hop_used = lax.broadcasted_iota(jnp.int32, (fan2, nodes), 0) < hop_counts[None, :]
    pick_nbr = pick_matrix(nbr_ids.T, hop_used, valid)
    pick_self = pick_matrix(self_ids[None, :], jnp.ones((1, nodes), bool), valid)
    hop_div = hop_counts.astype(f32)[:, None]
    seed_div = seed_counts.astype(f32)[:, None]

    used_two = (jnp.arange(fan1, dtype=jnp.int32)[None, :] < seed_counts[:, None]).astype(f32)
    back_self = contract(cotangent, w_self2, 1, 1)
    back_mean = contract(cotangent, w_nbr2, 1, 1) / seed_div
    back_hop = (back_mean[:, None, :] * used_two[:, :, None]).reshape(seeds * fan1, hidden)
    back_hidden = jnp.concatenate([back_self, back_hop], 0)

    own_rows = contract(pick_self, fetched, 0, 0).astype(bf16)
    mean_one = (contract(pick_nbr, fetched, 0, 0) / hop_div).astype(bf16)
    pre = jnp.dot(own_rows, w_self1, preferred_element_type=f32) + jnp.dot(
        mean_one, w_nbr1, preferred_element_type=f32
    )
    gate = jax.nn.sigmoid(pre)
    hidden_one = (pre * gate).astype(bf16)
    back_pre = (back_hidden * gate * (1.0 + pre * (1.0 - gate))).astype(bf16)

    place = lax.broadcasted_iota(jnp.int32, (seeds, nodes), 1) - seeds
    first = lax.broadcasted_iota(jnp.int32, (seeds, nodes), 0) * fan1
    pick_two = ((place >= first) & (place < first + seed_counts[:, None])).astype(bf16)
    seed_rows = hidden_one[:seeds]
    mean_two = (jnp.dot(pick_two, hidden_one, preferred_element_type=f32) / seed_div).astype(bf16)
    embedding = (
        jnp.dot(seed_rows, w_self2, preferred_element_type=f32)
        + jnp.dot(mean_two, w_nbr2, preferred_element_type=f32)
    ).astype(bf16)

    terms = jnp.concatenate(
        [contract(back_pre, own_rows, 0, 0).astype(bf16), contract(back_pre, mean_one, 0, 0).astype(bf16)], 1
    )
    terms = lax.all_to_all(
        terms.reshape(n_hst, n_dev, part, 2 * width_in), "dev", split_axis=1, concat_axis=1, tiled=True
    )
    sum_one = jnp.sum(terms.astype(f32), 1).astype(bf16)
    rows_two = lax.all_gather(jnp.concatenate([seed_rows, mean_two], 1), "dev", axis=0, tiled=True)
    sum_two = contract(cot_cols, rows_two, 0, 0).astype(bf16).reshape(n_hst, part, 2 * hidden)
    both = lax.all_to_all(
        jnp.concatenate([sum_one, sum_two], 2), "hst", split_axis=0, concat_axis=0, tiled=True
    )
    total = jnp.sum(both.astype(f32), 0)
    cuts = (0, width_in, 2 * width_in, 2 * width_in + hidden, 2 * width_in + 2 * hidden)
    grads = tuple(total[:, a:b].T for a, b in zip(cuts[:-1], cuts[1:]))
    return (embedding, new_cache[None], *grads)


def solution(mesh):
    return jax.shard_map(
        local,
        mesh=mesh,
        in_specs=(
            P(BOTH, None),
            P("hst", "dev", None),
            P("hst", "dev"),
            P(BOTH, None, None, None),
            P(BOTH, None, None),
            P(BOTH),
            P(BOTH, None),
            P(BOTH),
            P(BOTH),
            P(),
            P(),
            P(),
            P(),
            P(BOTH, None),
        ),
        out_specs=(
            P(BOTH, None),
            P("hst", "dev", None),
            P(None, BOTH),
            P(None, BOTH),
            P(None, BOTH),
            P(None, BOTH),
        ),
        check_vma=False,
    )
```

```python
import functools

import jax
import jax.numpy as jnp
from jax import lax
from jax.experimental import pallas as pl
from jax.experimental.pallas import tpu as pltpu
from jax.sharding import PartitionSpec as P

CSLOT = 2
BOTH = ("hst", "dev")


def pick_matrix(ids, used, valid, dtype=jnp.bfloat16):
    slots = valid.shape[0]
    slot = lax.broadcasted_iota(jnp.int32, (slots, ids.shape[1]), 0)
    named = jnp.where(used, ids, -1)
    total = jnp.zeros(slot.shape, jnp.float32)
    for k in range(ids.shape[0]):
        total = total + jnp.where(named[k][None, :] == slot, 1.0, 0.0)
    return jnp.where(valid[:, None], total, 0.0).astype(dtype)


def contract(left, right, dim_left, dim_right):
    return lax.dot_general(
        left, right, (((dim_left,), (dim_right,)), ((), ())), preferred_element_type=jnp.float32
    )


def plus(a, b):
    return a.astype(jnp.float32) + b.astype(jnp.float32)


def sum_kernel(n_hst, own_ref, nbr_ref, rows_ref, cot_ref, out_own, out_nbr, out_two,
               own_c, nbr_c, own_1, nbr_1, own_x, nbr_y, own_2, nbr_2, own_y, nbr_x, own_s, nbr_s,
               rows_all, two_s, own_z, nbr_z, two_z, send_sem, recv_sem):
    h, d = lax.axis_index("hst"), lax.axis_index("dev")
    y, x, c = d // 4, (d // 2) % 2, d % 2
    to_core = (h, y * 4 + x * 2 + 1 - c)
    to_x = (h, y * 4 + (1 - x) * 2 + c)
    to_y = (h, (1 - y) * 4 + x * 2 + c)
    to_diag = (h, (1 - y) * 4 + (1 - x) * 2 + c)
    to_hst = [((h + j) % n_hst, d) for j in range(1, n_hst)]
    peers = [to_core, to_x, to_y, to_diag] + to_hst

    barrier = pltpu.get_barrier_semaphore()
    for peer in peers:
        pl.semaphore_signal(barrier, inc=1, device_id=peer, device_id_type=pl.DeviceIdType.MESH)
    pl.semaphore_wait(barrier, len(peers))

    used = [0]

    def send(src, dst, peer):
        k = used[0]
        used[0] = k + 1
        copy = pltpu.make_async_remote_copy(
            src_ref=src, dst_ref=dst, send_sem=send_sem.at[k], recv_sem=recv_sem.at[k],
            device_id=peer, device_id_type=pl.DeviceIdType.MESH,
        )
        copy.start()
        return copy

    own_row = rows_all.at[d]
    rows_x = send(rows_ref, own_row, to_x)
    rows_y = send(rows_ref, own_row, to_y)
    core_own = send(own_ref.at[:, 1 - c], own_c, to_core)
    rows_diag = send(rows_ref, own_row, to_diag)
    core_nbr = send(nbr_ref.at[:, 1 - c], nbr_c, to_core)
    rows_core = [send(rows_ref, own_row, to_core)]
    rows_all[d] = rows_ref[...]

    part = own_ref.shape[2]
    bf16 = own_s.dtype
    count = own_ref.shape[0]

    core_own.wait()

    @pl.loop(0, count)
    def _(i):
        own_1[i // 2, i % 2] = plus(own_ref[i, c], own_c[i]).astype(bf16)

    x_own = send(own_1.at[:, 1 - x], own_x, to_x)
    core_nbr.wait()

    @pl.loop(0, count)
    def _(i):
        nbr_1[i // 4, (i // 2) % 2, i % 2] = plus(nbr_ref[i, c], nbr_c[i]).astype(bf16)

    y_nbr = send(nbr_1.at[:, 1 - y], nbr_y, to_y)

    for copy, peer in ((rows_x, to_x), (rows_y, to_y), (rows_diag, to_diag)):
        copy.wait()
        slot = rows_all.at[peer[1]]
        rows_core.append(send(slot, slot, to_core))
    for copy in rows_core:
        copy.wait()
    wide = rows_all.shape[2]
    gathered = rows_all.shape[0] * rows_all.shape[1]
    tile = 512

    @pl.loop(0, wide // tile)
    def _(t):
        cols = pl.ds(pl.multiple_of(t * tile, tile), tile)
        block = rows_all[:, :, cols].reshape(gathered, tile)
        prod = jnp.dot(cot_ref[...], block, preferred_element_type=jnp.float32)
        two_s[:, :, cols] = prod.astype(bf16).reshape(n_hst, part, tile)

    two_copies = [send(two_s.at[peer[0]], two_z.at[j], peer) for j, peer in enumerate(to_hst)]

    x_own.wait()

    @pl.loop(0, count // 2)
    def _(i):
        own_2[i // 2, i % 2] = plus(own_1[i, x], own_x[i]).astype(bf16)

    y_own = send(own_2.at[:, 1 - y], own_y, to_y)
    y_nbr.wait()

    @pl.loop(0, count // 2)
    def _(i):
        nbr_2[i // 2, i % 2] = plus(nbr_1[i // 2, y, i % 2], nbr_y[i // 2, i % 2]).astype(bf16)

    x_nbr = send(nbr_2.at[:, 1 - x], nbr_x, to_x)

    y_own.wait()

    @pl.loop(0, n_hst)
    def _(i):
        own_s[i] = plus(own_2[i, y], own_y[i]).astype(bf16)

    own_copies = [send(own_s.at[peer[0]], own_z.at[j], peer) for j, peer in enumerate(to_hst)]
    x_nbr.wait()

    @pl.loop(0, n_hst)
    def _(i):
        nbr_s[i] = plus(nbr_2[i, x], nbr_x[i]).astype(bf16)

    nbr_copies = [send(nbr_s.at[peer[0]], nbr_z.at[j], peer) for j, peer in enumerate(to_hst)]

    for copies, mine, landed, out in (
        (two_copies, two_s, two_z, out_two),
        (own_copies, own_s, own_z, out_own),
        (nbr_copies, nbr_s, nbr_z, out_nbr),
    ):
        for copy in copies:
            copy.wait()
        total = mine[h].astype(jnp.float32)
        for j in range(n_hst - 1):
            total = total + landed[j].astype(jnp.float32)
        out[...] = total


def sum_over_devices(n_hst, terms_own, terms_nbr, rows, cot_rows):
    hidden, width = terms_own.shape
    seeds, wide = rows.shape
    part = hidden // (n_hst * 8)
    bf16, f32 = jnp.bfloat16, jnp.float32
    count = n_hst * 4
    vmem = lambda *shape: pltpu.VMEM(shape, bf16)
    others = n_hst - 1
    copies = 13 + 3 * others
    return pl.pallas_call(
        functools.partial(sum_kernel, n_hst),
        out_shape=(
            jax.ShapeDtypeStruct((part, width), f32),
            jax.ShapeDtypeStruct((part, width), f32),
            jax.ShapeDtypeStruct((part, wide), f32),
        ),
        in_specs=[pl.BlockSpec(memory_space=pltpu.VMEM)] * 4,
        out_specs=[pl.BlockSpec(memory_space=pltpu.VMEM)] * 3,
        scratch_shapes=[
            vmem(count, part, width),
            vmem(count, part, width),
            vmem(count // 2, 2, part, width),
            vmem(n_hst, 2, 2, part, width),
            vmem(count // 2, part, width),
            vmem(n_hst, 2, part, width),
            vmem(n_hst, 2, part, width),
            vmem(n_hst, 2, part, width),
            vmem(n_hst, part, width),
            vmem(n_hst, part, width),
            vmem(n_hst, part, width),
            vmem(n_hst, part, width),
            vmem(8, seeds, wide),
            vmem(n_hst, part, wide),
            vmem(others, part, width),
            vmem(others, part, width),
            vmem(others, part, wide),
            pltpu.SemaphoreType.DMA((copies,)),
            pltpu.SemaphoreType.DMA((copies,)),
        ],
        compiler_params=pltpu.CompilerParams(
            collective_id=0, has_side_effects=True, vmem_limit_bytes=40 * 1024 * 1024
        ),
        cost_estimate=pl.CostEstimate(flops=2 * n_hst * part * 8 * seeds * wide, bytes_accessed=2 * hidden * width * 4, transcendentals=0),
        name="sum_over_devices",
    )(
        terms_own.reshape(count, 2, part, width),
        terms_nbr.reshape(count, 2, part, width),
        rows,
        cot_rows,
    )


def local(
    features,
    cache_blocks,
    plan,
    miss_ids,
    miss_counts,
    self_ids,
    nbr_ids,
    hop_counts,
    seed_counts,
    w_self1,
    w_nbr1,
    w_self2,
    w_nbr2,
    cotangent,
):
    bf16, f32 = jnp.bfloat16, jnp.float32
    home_rows, width_in = features.shape
    slot_count = miss_ids.shape[3]
    n_hst, n_dev = lax.axis_size("hst"), lax.axis_size("dev")
    device_count = n_hst * n_dev
    nodes, fan2 = nbr_ids.shape
    seeds = seed_counts.shape[0]
    fan1 = (nodes - seeds) // seeds
    hidden = w_self1.shape[1]
    part = hidden // device_count
    cache_rows = cache_blocks.shape[1]
    block = cache_rows // CSLOT

    everyones = lax.all_gather(cache_blocks[0], "dev", axis=0, tiled=True)
    requests = lax.all_to_all(
        miss_ids.reshape(device_count, slot_count), BOTH, split_axis=0, concat_axis=0, tiled=True
    ).reshape(-1)
    cot_parts = cotangent.reshape(seeds, n_hst, n_dev, part).transpose(2, 0, 1, 3)
    cot_cols = lax.all_to_all(
        cot_parts.reshape(n_dev, seeds, n_hst * part), "dev", split_axis=0, concat_axis=0, tiled=True
    ).reshape(n_dev * seeds, n_hst * part)

    requests, cot_cols = lax.optimization_barrier((requests, cot_cols))
    from_home = features[jnp.minimum(requests, home_rows - 1)]
    blocks = everyones.reshape(-1, block, width_in)
    new_cache = jnp.concatenate(
        [lax.dynamic_index_in_dim(blocks, plan[0, j], 0, keepdims=False) for j in range(CSLOT)], 0
    )
    row = lax.broadcasted_iota(jnp.int32, (cache_rows, requests.shape[0]), 0)
    in_cache = ((requests - home_rows)[None, :] == row).astype(bf16)
    from_cache = contract(in_cache, new_cache, 0, 0).astype(bf16)
    row_data = jnp.where((requests < home_rows)[:, None], from_home, from_cache)
    fetched = lax.all_to_all(
        row_data.reshape(device_count, slot_count, width_in), BOTH, split_axis=0, concat_axis=0, tiled=True
    ).reshape(device_count * slot_count, width_in)

    valid = (
        lax.broadcasted_iota(jnp.int32, (device_count, slot_count), 1)
        < miss_counts.reshape(device_count)[:, None]
    ).reshape(-1)
    hop_used = lax.broadcasted_iota(jnp.int32, (fan2, nodes), 0) < hop_counts[None, :]
    pick_nbr = pick_matrix(nbr_ids.T, hop_used, valid)
    pick_self = pick_matrix(self_ids[None, :], jnp.ones((1, nodes), bool), valid)
    pick_nbr, pick_self = lax.optimization_barrier((pick_nbr, pick_self))
    hop_div = hop_counts.astype(f32)[:, None]
    seed_div = seed_counts.astype(f32)[:, None]

    used_two = (jnp.arange(fan1, dtype=jnp.int32)[None, :] < seed_counts[:, None]).astype(f32)
    back_self = contract(cotangent, w_self2, 1, 1)
    back_mean = contract(cotangent, w_nbr2, 1, 1) / seed_div
    back_hop = (back_mean[:, None, :] * used_two[:, :, None]).reshape(seeds * fan1, hidden)
    back_hidden = jnp.concatenate([back_self, back_hop], 0)

    own_rows = contract(pick_self, fetched, 0, 0).astype(bf16)
    mean_one = (contract(pick_nbr, fetched, 0, 0) / hop_div).astype(bf16)
    pre = jnp.dot(own_rows, w_self1, preferred_element_type=f32) + jnp.dot(
        mean_one, w_nbr1, preferred_element_type=f32
    )
    gate = jax.nn.sigmoid(pre)
    hidden_one = (pre * gate).astype(bf16)
    back_pre = (back_hidden * gate * (1.0 + pre * (1.0 - gate))).astype(bf16)

    place = lax.broadcasted_iota(jnp.int32, (seeds, nodes), 1) - seeds
    first = lax.broadcasted_iota(jnp.int32, (seeds, nodes), 0) * fan1
    pick_two = ((place >= first) & (place < first + seed_counts[:, None])).astype(bf16)
    seed_rows = hidden_one[:seeds]
    mean_two = (jnp.dot(pick_two, hidden_one, preferred_element_type=f32) / seed_div).astype(bf16)
    embedding = (
        jnp.dot(seed_rows, w_self2, preferred_element_type=f32)
        + jnp.dot(mean_two, w_nbr2, preferred_element_type=f32)
    ).astype(bf16)

    terms_own = contract(back_pre, own_rows, 0, 0).astype(bf16)
    terms_nbr = contract(back_pre, mean_one, 0, 0).astype(bf16)
    rows_two = jnp.concatenate([seed_rows, mean_two], 1)
    if n_dev == 8:
        sum_own, sum_nbr, sum_two = sum_over_devices(n_hst, terms_own, terms_nbr, rows_two, cot_cols.T)
    else:
        terms = jnp.concatenate([terms_own, terms_nbr], 1).reshape(n_hst, n_dev, part, 2 * width_in)
        terms = lax.all_to_all(terms, "dev", split_axis=1, concat_axis=1, tiled=True)
        sum_one = jnp.sum(terms.astype(f32), 1).astype(bf16)
        rows_all = lax.all_gather(rows_two, "dev", axis=0, tiled=True)
        sum_two = contract(cot_cols, rows_all, 0, 0).astype(bf16).reshape(n_hst, part, 2 * hidden)
        both = lax.all_to_all(
            jnp.concatenate([sum_one, sum_two], 2), "hst", split_axis=0, concat_axis=0, tiled=True
        )
        total = jnp.sum(both.astype(f32), 0)
        sum_own, sum_nbr = total[:, :width_in], total[:, width_in : 2 * width_in]
        sum_two = total[:, 2 * width_in :]
    grads = (sum_own.T, sum_nbr.T, sum_two[:, :hidden].T, sum_two[:, hidden:].T)
    return (embedding, new_cache[None], *grads)


def solution(mesh):
    return jax.shard_map(
        local,
        mesh=mesh,
        in_specs=(
            P(BOTH, None),
            P("hst", "dev", None),
            P("hst", "dev"),
            P(BOTH, None, None, None),
            P(BOTH, None, None),
            P(BOTH),
            P(BOTH, None),
            P(BOTH),
            P(BOTH),
            P(),
            P(),
            P(),
            P(),
            P(BOTH, None),
        ),
        out_specs=(
            P(BOTH, None),
            P("hst", "dev", None),
            P(None, BOTH),
            P(None, BOTH),
            P(None, BOTH),
            P(None, BOTH),
        ),
        check_vma=False,
    )
```

```python
import functools

import jax
import jax.numpy as jnp
from jax import lax
from jax.experimental import pallas as pl
from jax.experimental.pallas import tpu as pltpu
from jax.sharding import PartitionSpec as P

CSLOT = 2
BOTH = ("hst", "dev")


def pick_matrix(ids, used, valid, dtype=jnp.bfloat16):
    slots = valid.shape[0]
    slot = lax.broadcasted_iota(jnp.int32, (slots, ids.shape[1]), 0)
    named = jnp.where(used, ids, -1)
    total = jnp.zeros(slot.shape, jnp.float32)
    for k in range(ids.shape[0]):
        total = total + jnp.where(named[k][None, :] == slot, 1.0, 0.0)
    return jnp.where(valid[:, None], total, 0.0).astype(dtype)


def contract(left, right, dim_left, dim_right):
    return lax.dot_general(
        left, right, (((dim_left,), (dim_right,)), ((), ())), preferred_element_type=jnp.float32
    )


def plus(a, b):
    return a.astype(jnp.float32) + b.astype(jnp.float32)


def sum_kernel(n_hst, own_ref, nbr_ref, rows_ref, cot_ref, out_own, out_nbr, out_two,
               own_c, nbr_c, own_1, nbr_1, own_x, nbr_y, own_2, nbr_2, own_y, nbr_x, own_s, nbr_s,
               rows_all, two_s, own_z, nbr_z, two_z, send_sem, recv_sem):
    h, d = lax.axis_index("hst"), lax.axis_index("dev")
    y, x, c = d // 4, (d // 2) % 2, d % 2
    to_core = (h, y * 4 + x * 2 + 1 - c)
    to_x = (h, y * 4 + (1 - x) * 2 + c)
    to_y = (h, (1 - y) * 4 + x * 2 + c)
    to_diag = (h, (1 - y) * 4 + (1 - x) * 2 + c)
    to_hst = [((h + j) % n_hst, d) for j in range(1, n_hst)]
    peers = [to_core, to_x, to_y, to_diag] + to_hst

    barrier = pltpu.get_barrier_semaphore()
    for peer in peers:
        pl.semaphore_signal(barrier, inc=1, device_id=peer, device_id_type=pl.DeviceIdType.MESH)
    pl.semaphore_wait(barrier, len(peers))

    used = [0]

    def send(src, dst, peer):
        k = used[0]
        used[0] = k + 1
        copy = pltpu.make_async_remote_copy(
            src_ref=src, dst_ref=dst, send_sem=send_sem.at[k], recv_sem=recv_sem.at[k],
            device_id=peer, device_id_type=pl.DeviceIdType.MESH,
        )
        copy.start()
        return copy

    own_row = rows_all.at[d]
    rows_x = send(rows_ref, own_row, to_x)
    rows_y = send(rows_ref, own_row, to_y)
    core_own = send(own_ref.at[:, 1 - c], own_c, to_core)
    rows_diag = send(rows_ref, own_row, to_diag)
    core_nbr = send(nbr_ref.at[:, 1 - c], nbr_c, to_core)
    rows_core = [send(rows_ref, own_row, to_core)]
    rows_all[d] = rows_ref[...]

    part = own_ref.shape[2]
    bf16 = own_s.dtype
    count = own_ref.shape[0]

    core_own.wait()

    @pl.loop(0, count)
    def _(i):
        own_1[i // 2, i % 2] = plus(own_ref[i, c], own_c[i]).astype(bf16)

    x_own = send(own_1.at[:, 1 - x], own_x, to_x)
    core_nbr.wait()

    @pl.loop(0, count)
    def _(i):
        nbr_1[i // 4, (i // 2) % 2, i % 2] = plus(nbr_ref[i, c], nbr_c[i]).astype(bf16)

    y_nbr = send(nbr_1.at[:, 1 - y], nbr_y, to_y)

    for copy, peer in ((rows_x, to_x), (rows_y, to_y), (rows_diag, to_diag)):
        copy.wait()
        slot = rows_all.at[peer[1]]
        rows_core.append(send(slot, slot, to_core))
    for copy in rows_core:
        copy.wait()
    wide = rows_all.shape[2]
    gathered = rows_all.shape[0] * rows_all.shape[1]
    tile = 512

    @pl.loop(0, wide // tile)
    def _(t):
        cols = pl.ds(pl.multiple_of(t * tile, tile), tile)
        block = rows_all[:, :, cols].reshape(gathered, tile)
        prod = jnp.dot(cot_ref[...], block, preferred_element_type=jnp.float32)
        two_s[:, :, cols] = prod.astype(bf16).reshape(n_hst, part, tile)

    two_copies = [send(two_s.at[peer[0]], two_z.at[j], peer) for j, peer in enumerate(to_hst)]

    x_own.wait()

    @pl.loop(0, count // 2)
    def _(i):
        own_2[i // 2, i % 2] = plus(own_1[i, x], own_x[i]).astype(bf16)

    y_own = send(own_2.at[:, 1 - y], own_y, to_y)
    y_nbr.wait()

    @pl.loop(0, count // 2)
    def _(i):
        nbr_2[i // 2, i % 2] = plus(nbr_1[i // 2, y, i % 2], nbr_y[i // 2, i % 2]).astype(bf16)

    x_nbr = send(nbr_2.at[:, 1 - x], nbr_x, to_x)

    y_own.wait()

    @pl.loop(0, n_hst)
    def _(i):
        own_s[i] = plus(own_2[i, y], own_y[i]).astype(bf16)

    own_copies = [send(own_s.at[peer[0]], own_z.at[j], peer) for j, peer in enumerate(to_hst)]
    x_nbr.wait()

    @pl.loop(0, n_hst)
    def _(i):
        nbr_s[i] = plus(nbr_2[i, x], nbr_x[i]).astype(bf16)

    nbr_copies = [send(nbr_s.at[peer[0]], nbr_z.at[j], peer) for j, peer in enumerate(to_hst)]

    for copies, mine, landed, out in (
        (two_copies, two_s, two_z, out_two),
        (own_copies, own_s, own_z, out_own),
        (nbr_copies, nbr_s, nbr_z, out_nbr),
    ):
        for copy in copies:
            copy.wait()
        total = mine[h].astype(jnp.float32)
        for j in range(n_hst - 1):
            total = total + landed[j].astype(jnp.float32)
        out[...] = total


def sum_over_devices(n_hst, terms_own, terms_nbr, rows, cot_rows):
    hidden, width = terms_own.shape
    seeds, wide = rows.shape
    part = hidden // (n_hst * 8)
    bf16, f32 = jnp.bfloat16, jnp.float32
    count = n_hst * 4
    vmem = lambda *shape: pltpu.VMEM(shape, bf16)
    others = n_hst - 1
    copies = 13 + 3 * others
    return pl.pallas_call(
        functools.partial(sum_kernel, n_hst),
        out_shape=(
            jax.ShapeDtypeStruct((part, width), f32),
            jax.ShapeDtypeStruct((part, width), f32),
            jax.ShapeDtypeStruct((part, wide), f32),
        ),
        in_specs=[pl.BlockSpec(memory_space=pltpu.VMEM)] * 4,
        out_specs=[pl.BlockSpec(memory_space=pltpu.VMEM)] * 3,
        scratch_shapes=[
            vmem(count, part, width),
            vmem(count, part, width),
            vmem(count // 2, 2, part, width),
            vmem(n_hst, 2, 2, part, width),
            vmem(count // 2, part, width),
            vmem(n_hst, 2, part, width),
            vmem(n_hst, 2, part, width),
            vmem(n_hst, 2, part, width),
            vmem(n_hst, part, width),
            vmem(n_hst, part, width),
            vmem(n_hst, part, width),
            vmem(n_hst, part, width),
            vmem(8, seeds, wide),
            vmem(n_hst, part, wide),
            vmem(others, part, width),
            vmem(others, part, width),
            vmem(others, part, wide),
            pltpu.SemaphoreType.DMA((copies,)),
            pltpu.SemaphoreType.DMA((copies,)),
        ],
        compiler_params=pltpu.CompilerParams(
            collective_id=0, has_side_effects=True, vmem_limit_bytes=40 * 1024 * 1024
        ),
        cost_estimate=pl.CostEstimate(flops=2 * n_hst * part * 8 * seeds * wide, bytes_accessed=2 * hidden * width * 4, transcendentals=0),
        name="sum_over_devices",
    )(
        terms_own.reshape(count, 2, part, width),
        terms_nbr.reshape(count, 2, part, width),
        rows,
        cot_rows,
    )


def serve_kernel(plan_ref, cache_ref, home_ref, asked_ref, cot_ref, new_ref, rows_ref, cots_ref,
                 blocks, send_sem, recv_sem):
    h, d = lax.axis_index("hst"), lax.axis_index("dev")
    y, x, c = d // 4, (d // 2) % 2, d % 2
    place = lambda a, b, e: a * 4 + b * 2 + e
    to_core, to_x, to_y = place(y, x, 1 - c), place(y, 1 - x, c), place(1 - y, x, c)
    to_diag = place(1 - y, 1 - x, c)
    peers = [(d + j) % 8 for j in range(1, 8)]

    barrier = pltpu.get_barrier_semaphore()
    for peer in peers:
        pl.semaphore_signal(barrier, inc=1, device_id=(h, peer), device_id_type=pl.DeviceIdType.MESH)
    pl.semaphore_wait(barrier, len(peers))

    used = [0]

    def send(src, dst, peer):
        k = used[0]
        used[0] = k + 1
        copy = pltpu.make_async_remote_copy(
            src_ref=src, dst_ref=dst, send_sem=send_sem.at[k], recv_sem=recv_sem.at[k],
            device_id=(h, peer), device_id_type=pl.DeviceIdType.MESH,
        )
        copy.start()
        return copy

    def pass_on(owner, j, peer):
        slot = blocks.at[owner * CSLOT + j]
        return send(slot, slot, peer)

    own = lambda j, peer: send(cache_ref.at[j], blocks.at[d * CSLOT + j], peer)
    x_first, y_last = own(0, to_x), own(1, to_y)
    x_last, y_first = own(1, to_x), own(0, to_y)
    core = [own(0, to_core), own(1, to_core)]
    cots = [send(cot_ref.at[peer], cots_ref.at[d], peer) for peer in peers]
    for j in range(CSLOT):
        blocks[d * CSLOT + j] = cache_ref[j]
    cots_ref[d] = cot_ref[d]

    home_rows = home_ref.shape[0]
    asked_rows = asked_ref.shape[0]
    tile = 256
    tiles = asked_rows // tile
    bf16 = rows_ref.dtype

    def one_hot(rows, first, count):
        at = lax.broadcasted_iota(jnp.int32, (tile, count), 1) + first
        return jnp.where(asked_ref[rows, :] == at, 1.0, 0.0).astype(bf16)

    def from_home(t):
        rows = pl.ds(pl.multiple_of(t * tile, tile), tile)
        picked = jnp.dot(one_hot(rows, 0, home_rows), home_ref[...], preferred_element_type=jnp.float32)
        rows_ref[rows, :] = picked.astype(bf16)

    pl.loop(0, tiles // 2)(from_home)

    x_first.wait()
    diag_first = pass_on(to_x, 0, to_y)
    y_last.wait()
    diag_last = pass_on(to_y, 1, to_x)
    core += [pass_on(to_x, 0, to_core), pass_on(to_y, 1, to_core)]
    x_last.wait()
    core.append(pass_on(to_x, 1, to_core))
    y_first.wait()
    core.append(pass_on(to_y, 0, to_core))

    pl.loop(tiles // 2, tiles)(from_home)

    diag_first.wait()
    core.append(pass_on(to_diag, 0, to_core))
    diag_last.wait()
    core.append(pass_on(to_diag, 1, to_core))
    for copy in core + cots:
        copy.wait()

    block = cache_ref.shape[1]
    for j in range(CSLOT):
        new_ref[pl.ds(j * block, block), :] = blocks[plan_ref[0, j]]

    @pl.loop(0, tiles)
    def _(t):
        rows = pl.ds(pl.multiple_of(t * tile, tile), tile)
        hot = one_hot(rows, home_rows, CSLOT * block)
        picked = jnp.dot(hot, new_ref[...], preferred_element_type=jnp.float32)
        rows_ref[rows, :] = (rows_ref[rows, :].astype(jnp.float32) + picked).astype(bf16)


def serve_rows(plan, cache, home, asked, cot_parts):
    _, block, width = cache.shape
    bf16 = jnp.bfloat16
    asks = asked.shape[0]
    vmem = pl.BlockSpec(memory_space=pltpu.VMEM)
    copies = 21
    return pl.pallas_call(
        serve_kernel,
        out_shape=(
            jax.ShapeDtypeStruct((CSLOT * block, width), bf16),
            jax.ShapeDtypeStruct((asks, width), bf16),
            jax.ShapeDtypeStruct(cot_parts.shape, bf16),
        ),
        in_specs=[pl.BlockSpec(memory_space=pltpu.SMEM)] + [vmem] * 4,
        out_specs=[vmem] * 3,
        scratch_shapes=[
            pltpu.VMEM((8 * CSLOT, block, width), bf16),
            pltpu.SemaphoreType.DMA((copies,)),
            pltpu.SemaphoreType.DMA((copies,)),
        ],
        compiler_params=pltpu.CompilerParams(
            collective_id=1, has_side_effects=True, vmem_limit_bytes=40 * 1024 * 1024
        ),
        cost_estimate=pl.CostEstimate(
            flops=2 * asks * (home.shape[0] + CSLOT * block) * width,
            bytes_accessed=4 * (asks + home.shape[0]) * width,
            transcendentals=0,
        ),
        name="serve_rows",
    )(plan, cache, home, asked, cot_parts)


def local(
    features,
    cache_blocks,
    plan,
    miss_ids,
    miss_counts,
    self_ids,
    nbr_ids,
    hop_counts,
    seed_counts,
    w_self1,
    w_nbr1,
    w_self2,
    w_nbr2,
    cotangent,
):
    bf16, f32 = jnp.bfloat16, jnp.float32
    home_rows, width_in = features.shape
    slot_count = miss_ids.shape[3]
    n_hst, n_dev = lax.axis_size("hst"), lax.axis_size("dev")
    device_count = n_hst * n_dev
    nodes, fan2 = nbr_ids.shape
    seeds = seed_counts.shape[0]
    fan1 = (nodes - seeds) // seeds
    hidden = w_self1.shape[1]
    part = hidden // device_count
    cache_rows = cache_blocks.shape[1]
    block = cache_rows // CSLOT

    requests = lax.all_to_all(
        miss_ids.reshape(device_count, slot_count), BOTH, split_axis=0, concat_axis=0, tiled=True
    ).reshape(-1)
    cot_parts = cotangent.reshape(seeds, n_hst, n_dev, part).transpose(2, 0, 1, 3)
    cot_parts = cot_parts.reshape(n_dev, seeds, n_hst * part)
    if n_dev == 8:
        new_cache, row_data, cot_cols = serve_rows(
            plan, cache_blocks.reshape(CSLOT, block, width_in), features, requests[:, None], cot_parts
        )
        cot_cols = cot_cols.reshape(n_dev * seeds, n_hst * part)
    else:
        everyones = lax.all_gather(cache_blocks[0], "dev", axis=0, tiled=True)
        cot_cols = lax.all_to_all(
            cot_parts, "dev", split_axis=0, concat_axis=0, tiled=True
        ).reshape(n_dev * seeds, n_hst * part)
        from_home = features[jnp.minimum(requests, home_rows - 1)]
        blocks = everyones.reshape(-1, block, width_in)
        new_cache = jnp.concatenate(
            [lax.dynamic_index_in_dim(blocks, plan[0, j], 0, keepdims=False) for j in range(CSLOT)], 0
        )
        row = lax.broadcasted_iota(jnp.int32, (cache_rows, requests.shape[0]), 0)
        in_cache = ((requests - home_rows)[None, :] == row).astype(bf16)
        from_cache = contract(in_cache, new_cache, 0, 0).astype(bf16)
        row_data = jnp.where((requests < home_rows)[:, None], from_home, from_cache)
    fetched = lax.all_to_all(
        row_data.reshape(device_count, slot_count, width_in), BOTH, split_axis=0, concat_axis=0, tiled=True
    ).reshape(device_count * slot_count, width_in)

    valid = (
        lax.broadcasted_iota(jnp.int32, (device_count, slot_count), 1)
        < miss_counts.reshape(device_count)[:, None]
    ).reshape(-1)
    hop_used = lax.broadcasted_iota(jnp.int32, (fan2, nodes), 0) < hop_counts[None, :]
    pick_nbr = pick_matrix(nbr_ids.T, hop_used, valid)
    pick_self = pick_matrix(self_ids[None, :], jnp.ones((1, nodes), bool), valid)
    pick_nbr, pick_self = lax.optimization_barrier((pick_nbr.T, pick_self.T))
    hop_div = hop_counts.astype(f32)[:, None]
    seed_div = seed_counts.astype(f32)[:, None]

    used_two = (jnp.arange(fan1, dtype=jnp.int32)[None, :] < seed_counts[:, None]).astype(f32)
    back_self = contract(cotangent, w_self2, 1, 1)
    back_mean = contract(cotangent, w_nbr2, 1, 1) / seed_div
    back_hop = (back_mean[:, None, :] * used_two[:, :, None]).reshape(seeds * fan1, hidden)
    back_hidden = jnp.concatenate([back_self, back_hop], 0)

    own_rows = contract(pick_self, fetched, 1, 0).astype(bf16)
    mean_one = (contract(pick_nbr, fetched, 1, 0) / hop_div).astype(bf16)
    pre = jnp.dot(own_rows, w_self1, preferred_element_type=f32) + jnp.dot(
        mean_one, w_nbr1, preferred_element_type=f32
    )
    gate = jax.nn.sigmoid(pre)
    hidden_one = (pre * gate).astype(bf16)
    back_pre = (back_hidden * gate * (1.0 + pre * (1.0 - gate))).astype(bf16)

    place = lax.broadcasted_iota(jnp.int32, (seeds, nodes), 1) - seeds
    first = lax.broadcasted_iota(jnp.int32, (seeds, nodes), 0) * fan1
    pick_two = ((place >= first) & (place < first + seed_counts[:, None])).astype(bf16)
    seed_rows = hidden_one[:seeds]
    mean_two = (jnp.dot(pick_two, hidden_one, preferred_element_type=f32) / seed_div).astype(bf16)
    embedding = (
        jnp.dot(seed_rows, w_self2, preferred_element_type=f32)
        + jnp.dot(mean_two, w_nbr2, preferred_element_type=f32)
    ).astype(bf16)

    terms_own = contract(back_pre, own_rows, 0, 0).astype(bf16)
    terms_nbr = contract(back_pre, mean_one, 0, 0).astype(bf16)
    rows_two = jnp.concatenate([seed_rows, mean_two], 1)
    if n_dev == 8:
        sum_own, sum_nbr, sum_two = sum_over_devices(n_hst, terms_own, terms_nbr, rows_two, cot_cols.T)
    else:
        terms = jnp.concatenate([terms_own, terms_nbr], 1).reshape(n_hst, n_dev, part, 2 * width_in)
        terms = lax.all_to_all(terms, "dev", split_axis=1, concat_axis=1, tiled=True)
        sum_one = jnp.sum(terms.astype(f32), 1).astype(bf16)
        rows_all = lax.all_gather(rows_two, "dev", axis=0, tiled=True)
        sum_two = contract(cot_cols, rows_all, 0, 0).astype(bf16).reshape(n_hst, part, 2 * hidden)
        both = lax.all_to_all(
            jnp.concatenate([sum_one, sum_two], 2), "hst", split_axis=0, concat_axis=0, tiled=True
        )
        total = jnp.sum(both.astype(f32), 0)
        sum_own, sum_nbr = total[:, :width_in], total[:, width_in : 2 * width_in]
        sum_two = total[:, 2 * width_in :]
    grads = (sum_own.T, sum_nbr.T, sum_two[:, :hidden].T, sum_two[:, hidden:].T)
    return (embedding, new_cache[None], *grads)


def solution(mesh):
    return jax.shard_map(
        local,
        mesh=mesh,
        in_specs=(
            P(BOTH, None),
            P("hst", "dev", None),
            P("hst", "dev"),
            P(BOTH, None, None, None),
            P(BOTH, None, None),
            P(BOTH),
            P(BOTH, None),
            P(BOTH),
            P(BOTH),
            P(),
            P(),
            P(),
            P(),
            P(BOTH, None),
        ),
        out_specs=(
            P(BOTH, None),
            P("hst", "dev", None),
            P(None, BOTH),
            P(None, BOTH),
            P(None, BOTH),
            P(None, BOTH),
        ),
        check_vma=False,
    )
```

```python
import functools

import jax
import jax.numpy as jnp
from jax import lax
from jax.experimental import pallas as pl
from jax.experimental.pallas import tpu as pltpu
from jax.sharding import PartitionSpec as P

CSLOT = 2
BOTH = ("hst", "dev")


def pick_matrix(ids, used, valid, dtype=jnp.bfloat16):
    slots = valid.shape[0]
    slot = lax.broadcasted_iota(jnp.int32, (slots, ids.shape[1]), 0)
    named = jnp.where(used, ids, -1)
    total = jnp.zeros(slot.shape, jnp.float32)
    for k in range(ids.shape[0]):
        total = total + jnp.where(named[k][None, :] == slot, 1.0, 0.0)
    return jnp.where(valid[:, None], total, 0.0).astype(dtype)


def contract(left, right, dim_left, dim_right):
    return lax.dot_general(
        left, right, (((dim_left,), (dim_right,)), ((), ())), preferred_element_type=jnp.float32
    )


def plus(a, b):
    return a.astype(jnp.float32) + b.astype(jnp.float32)


def sum_kernel(n_hst, own_ref, nbr_ref, rows_ref, cot_ref, out_own, out_nbr, out_two,
               own_c, nbr_c, own_1, nbr_1, own_x, nbr_y, own_2, nbr_2, own_y, nbr_x, own_s, nbr_s,
               rows_all, two_s, own_z, nbr_z, two_z, send_sem, recv_sem):
    h, d = lax.axis_index("hst"), lax.axis_index("dev")
    y, x, c = d // 4, (d // 2) % 2, d % 2
    to_core = (h, y * 4 + x * 2 + 1 - c)
    to_x = (h, y * 4 + (1 - x) * 2 + c)
    to_y = (h, (1 - y) * 4 + x * 2 + c)
    to_diag = (h, (1 - y) * 4 + (1 - x) * 2 + c)
    to_hst = [((h + j) % n_hst, d) for j in range(1, n_hst)]
    peers = [to_core, to_x, to_y, to_diag] + to_hst

    barrier = pltpu.get_barrier_semaphore()
    for peer in peers:
        pl.semaphore_signal(barrier, inc=1, device_id=peer, device_id_type=pl.DeviceIdType.MESH)
    pl.semaphore_wait(barrier, len(peers))

    used = [0]

    def send(src, dst, peer):
        k = used[0]
        used[0] = k + 1
        copy = pltpu.make_async_remote_copy(
            src_ref=src, dst_ref=dst, send_sem=send_sem.at[k], recv_sem=recv_sem.at[k],
            device_id=peer, device_id_type=pl.DeviceIdType.MESH,
        )
        copy.start()
        return copy

    own_row = rows_all.at[d]
    rows_x = send(rows_ref, own_row, to_x)
    rows_y = send(rows_ref, own_row, to_y)
    core_own = send(own_ref.at[:, 1 - c], own_c, to_core)
    rows_diag = send(rows_ref, own_row, to_diag)
    core_nbr = send(nbr_ref.at[:, 1 - c], nbr_c, to_core)
    rows_core = [send(rows_ref, own_row, to_core)]
    rows_all[d] = rows_ref[...]

    part = own_ref.shape[2]
    bf16 = own_s.dtype
    count = own_ref.shape[0]

    core_own.wait()

    @pl.loop(0, count)
    def _(i):
        own_1[i // 2, i % 2] = plus(own_ref[i, c], own_c[i]).astype(bf16)

    x_own = send(own_1.at[:, 1 - x], own_x, to_x)
    core_nbr.wait()

    @pl.loop(0, count)
    def _(i):
        nbr_1[i // 4, (i // 2) % 2, i % 2] = plus(nbr_ref[i, c], nbr_c[i]).astype(bf16)

    y_nbr = send(nbr_1.at[:, 1 - y], nbr_y, to_y)

    for copy, peer in ((rows_x, to_x), (rows_y, to_y), (rows_diag, to_diag)):
        copy.wait()
        slot = rows_all.at[peer[1]]
        rows_core.append(send(slot, slot, to_core))
    for copy in rows_core:
        copy.wait()
    wide = rows_all.shape[2]
    gathered = rows_all.shape[0] * rows_all.shape[1]
    tile = 512

    @pl.loop(0, wide // tile)
    def _(t):
        cols = pl.ds(pl.multiple_of(t * tile, tile), tile)
        block = rows_all[:, :, cols].reshape(gathered, tile)
        prod = jnp.dot(cot_ref[...], block, preferred_element_type=jnp.float32)
        two_s[:, :, cols] = prod.astype(bf16).reshape(n_hst, part, tile)

    two_copies = [send(two_s.at[peer[0]], two_z.at[j], peer) for j, peer in enumerate(to_hst)]

    x_own.wait()

    @pl.loop(0, count // 2)
    def _(i):
        own_2[i // 2, i % 2] = plus(own_1[i, x], own_x[i]).astype(bf16)

    y_own = send(own_2.at[:, 1 - y], own_y, to_y)
    y_nbr.wait()

    @pl.loop(0, count // 2)
    def _(i):
        nbr_2[i // 2, i % 2] = plus(nbr_1[i // 2, y, i % 2], nbr_y[i // 2, i % 2]).astype(bf16)

    x_nbr = send(nbr_2.at[:, 1 - x], nbr_x, to_x)

    y_own.wait()

    @pl.loop(0, n_hst)
    def _(i):
        own_s[i] = plus(own_2[i, y], own_y[i]).astype(bf16)

    own_copies = [send(own_s.at[peer[0]], own_z.at[j], peer) for j, peer in enumerate(to_hst)]
    x_nbr.wait()

    @pl.loop(0, n_hst)
    def _(i):
        nbr_s[i] = plus(nbr_2[i, x], nbr_x[i]).astype(bf16)

    nbr_copies = [send(nbr_s.at[peer[0]], nbr_z.at[j], peer) for j, peer in enumerate(to_hst)]

    for copies, mine, landed, out in (
        (two_copies, two_s, two_z, out_two),
        (own_copies, own_s, own_z, out_own),
        (nbr_copies, nbr_s, nbr_z, out_nbr),
    ):
        for copy in copies:
            copy.wait()
        total = mine[h].astype(jnp.float32)
        for j in range(n_hst - 1):
            total = total + landed[j].astype(jnp.float32)
        out[...] = total


def sum_over_devices(n_hst, terms_own, terms_nbr, rows, cot_rows):
    hidden, width = terms_own.shape
    seeds, wide = rows.shape
    part = hidden // (n_hst * 8)
    bf16, f32 = jnp.bfloat16, jnp.float32
    count = n_hst * 4
    vmem = lambda *shape: pltpu.VMEM(shape, bf16)
    others = n_hst - 1
    copies = 13 + 3 * others
    return pl.pallas_call(
        functools.partial(sum_kernel, n_hst),
        out_shape=(
            jax.ShapeDtypeStruct((part, width), f32),
            jax.ShapeDtypeStruct((part, width), f32),
            jax.ShapeDtypeStruct((part, wide), f32),
        ),
        in_specs=[pl.BlockSpec(memory_space=pltpu.VMEM)] * 4,
        out_specs=[pl.BlockSpec(memory_space=pltpu.VMEM)] * 3,
        scratch_shapes=[
            vmem(count, part, width),
            vmem(count, part, width),
            vmem(count // 2, 2, part, width),
            vmem(n_hst, 2, 2, part, width),
            vmem(count // 2, part, width),
            vmem(n_hst, 2, part, width),
            vmem(n_hst, 2, part, width),
            vmem(n_hst, 2, part, width),
            vmem(n_hst, part, width),
            vmem(n_hst, part, width),
            vmem(n_hst, part, width),
            vmem(n_hst, part, width),
            vmem(8, seeds, wide),
            vmem(n_hst, part, wide),
            vmem(others, part, width),
            vmem(others, part, width),
            vmem(others, part, wide),
            pltpu.SemaphoreType.DMA((copies,)),
            pltpu.SemaphoreType.DMA((copies,)),
        ],
        compiler_params=pltpu.CompilerParams(
            collective_id=0, has_side_effects=True, vmem_limit_bytes=40 * 1024 * 1024
        ),
        cost_estimate=pl.CostEstimate(flops=2 * n_hst * part * 8 * seeds * wide, bytes_accessed=2 * hidden * width * 4, transcendentals=0),
        name="sum_over_devices",
    )(
        terms_own.reshape(count, 2, part, width),
        terms_nbr.reshape(count, 2, part, width),
        rows,
        cot_rows,
    )


def serve_kernel(n_hst, plan_ref, cache_ref, home_hbm, ask_ref, cot_ref, new_ref, rows_ref, cots_ref,
                 blocks, home_ref, asked_ref, home_sem, send_sem, recv_sem):
    home_copy = pltpu.make_async_copy(home_hbm, home_ref, home_sem)
    home_copy.start()
    h, d = lax.axis_index("hst"), lax.axis_index("dev")
    y, x, c = d // 4, (d // 2) % 2, d % 2
    place = lambda a, b, e: a * 4 + b * 2 + e
    to_core, to_x, to_y = place(y, x, 1 - c), place(y, 1 - x, c), place(1 - y, x, c)
    to_diag = place(1 - y, 1 - x, c)
    peers = [(d + j) % 8 for j in range(1, 8)]
    me = h * 8 + d
    everyone = [(me + j) % (n_hst * 8) for j in range(1, n_hst * 8)]

    barrier = pltpu.get_barrier_semaphore()
    for q in everyone:
        pl.semaphore_signal(
            barrier, inc=1, device_id=(q // 8, q % 8), device_id_type=pl.DeviceIdType.MESH
        )
    pl.semaphore_wait(barrier, len(everyone))

    used = [0]

    def send(src, dst, peer, plane=h):
        k = used[0]
        used[0] = k + 1
        copy = pltpu.make_async_remote_copy(
            src_ref=src, dst_ref=dst, send_sem=send_sem.at[k], recv_sem=recv_sem.at[k],
            device_id=(plane, peer), device_id_type=pl.DeviceIdType.MESH,
        )
        copy.start()
        return copy

    def pass_on(owner, j, peer):
        slot = blocks.at[owner * CSLOT + j]
        return send(slot, slot, peer)

    own = lambda j, peer: send(cache_ref.at[j], blocks.at[d * CSLOT + j], peer)
    x_first, y_last = own(0, to_x), own(1, to_y)
    x_last, y_first = own(1, to_x), own(0, to_y)
    asks = [send(ask_ref.at[q], asked_ref.at[me], q % 8, q // 8) for q in everyone]
    core = [own(0, to_core), own(1, to_core)]
    cots = [send(cot_ref.at[peer], cots_ref.at[d], peer) for peer in peers]
    for j in range(CSLOT):
        blocks[d * CSLOT + j] = cache_ref[j]
    cots_ref[d] = cot_ref[d]
    asked_ref[me] = ask_ref[me]

    home_rows = home_ref.shape[0]
    slots = ask_ref.shape[2]
    together = 4
    tile = together * slots
    tiles = asked_ref.shape[0] // together
    bf16 = rows_ref.dtype
    diagonal = lax.broadcasted_iota(jnp.int32, (slots, slots), 0) == lax.broadcasted_iota(
        jnp.int32, (slots, slots), 1
    )

    def column(p):
        row = jnp.broadcast_to(asked_ref[p].astype(jnp.float32), (slots, slots))
        return jnp.sum(jnp.where(diagonal, row, 0.0), axis=1, keepdims=True)

    def one_hot(t, first, count):
        asked = jnp.concatenate([column(t * together + u) for u in range(together)], 0)
        at = lax.broadcasted_iota(jnp.int32, (tile, count), 1) + first
        return jnp.where(asked == at.astype(jnp.float32), 1.0, 0.0).astype(bf16)

    home_copy.wait()
    for copy in asks:
        copy.wait()

    def from_home(t):
        rows = pl.ds(pl.multiple_of(t * tile, tile), tile)
        picked = jnp.dot(one_hot(t, 0, home_rows), home_ref[...], preferred_element_type=jnp.float32)
        rows_ref[rows, :] = picked.astype(bf16)

    pl.loop(0, tiles // 2)(from_home)

    x_first.wait()
    diag_first = pass_on(to_x, 0, to_y)
    y_last.wait()
    diag_last = pass_on(to_y, 1, to_x)
    core += [pass_on(to_x, 0, to_core), pass_on(to_y, 1, to_core)]
    x_last.wait()
    core.append(pass_on(to_x, 1, to_core))
    y_first.wait()
    core.append(pass_on(to_y, 0, to_core))

    pl.loop(tiles // 2, tiles)(from_home)

    diag_first.wait()
    core.append(pass_on(to_diag, 0, to_core))
    diag_last.wait()
    core.append(pass_on(to_diag, 1, to_core))
    for copy in core + cots:
        copy.wait()

    block = cache_ref.shape[1]
    for j in range(CSLOT):
        new_ref[pl.ds(j * block, block), :] = blocks[plan_ref[0, j]]

    @pl.loop(0, tiles)
    def _(t):
        rows = pl.ds(pl.multiple_of(t * tile, tile), tile)
        hot = one_hot(t, home_rows, CSLOT * block)
        picked = jnp.dot(hot, new_ref[...], preferred_element_type=jnp.float32)
        rows_ref[rows, :] = (rows_ref[rows, :].astype(jnp.float32) + picked).astype(bf16)


def serve_rows(n_hst, plan, cache, home, ask, cot_parts):
    _, block, width = cache.shape
    bf16 = jnp.bfloat16
    asks = ask.shape[0] * ask.shape[2]
    vmem = pl.BlockSpec(memory_space=pltpu.VMEM)
    copies = 20 + ask.shape[0]
    return pl.pallas_call(
        functools.partial(serve_kernel, n_hst),
        out_shape=(
            jax.ShapeDtypeStruct((CSLOT * block, width), bf16),
            jax.ShapeDtypeStruct((asks, width), bf16),
            jax.ShapeDtypeStruct(cot_parts.shape, bf16),
        ),
        in_specs=[pl.BlockSpec(memory_space=pltpu.SMEM), vmem, pl.BlockSpec(memory_space=pl.ANY), vmem, vmem],
        out_specs=[vmem] * 3,
        scratch_shapes=[
            pltpu.VMEM((8 * CSLOT, block, width), bf16),
            pltpu.VMEM(home.shape, bf16),
            pltpu.VMEM(ask.shape, jnp.int32),
            pltpu.SemaphoreType.DMA,
            pltpu.SemaphoreType.DMA((copies,)),
            pltpu.SemaphoreType.DMA((copies,)),
        ],
        compiler_params=pltpu.CompilerParams(
            collective_id=1, has_side_effects=True, vmem_limit_bytes=40 * 1024 * 1024
        ),
        cost_estimate=pl.CostEstimate(
            flops=2 * asks * (home.shape[0] + CSLOT * block) * width,
            bytes_accessed=4 * (asks + home.shape[0]) * width,
            transcendentals=0,
        ),
        name="serve_rows",
    )(plan, cache, home, ask, cot_parts)


def local(
    features,
    cache_blocks,
    plan,
    miss_ids,
    miss_counts,
    self_ids,
    nbr_ids,
    hop_counts,
    seed_counts,
    w_self1,
    w_nbr1,
    w_self2,
    w_nbr2,
    cotangent,
):
    bf16, f32 = jnp.bfloat16, jnp.float32
    home_rows, width_in = features.shape
    slot_count = miss_ids.shape[3]
    n_hst, n_dev = lax.axis_size("hst"), lax.axis_size("dev")
    device_count = n_hst * n_dev
    nodes, fan2 = nbr_ids.shape
    seeds = seed_counts.shape[0]
    fan1 = (nodes - seeds) // seeds
    hidden = w_self1.shape[1]
    part = hidden // device_count
    cache_rows = cache_blocks.shape[1]
    block = cache_rows // CSLOT

    cot_parts = cotangent.reshape(seeds, n_hst, n_dev, part).transpose(2, 0, 1, 3)
    cot_parts = cot_parts.reshape(n_dev, seeds, n_hst * part)
    if n_dev == 8:
        new_cache, row_data, cot_cols = serve_rows(
            n_hst,
            plan,
            cache_blocks.reshape(CSLOT, block, width_in),
            features,
            miss_ids.reshape(device_count, 1, slot_count),
            cot_parts,
        )
        cot_cols = cot_cols.reshape(n_dev * seeds, n_hst * part)
    else:
        everyones = lax.all_gather(cache_blocks[0], "dev", axis=0, tiled=True)
        cot_cols = lax.all_to_all(
            cot_parts, "dev", split_axis=0, concat_axis=0, tiled=True
        ).reshape(n_dev * seeds, n_hst * part)
        requests = lax.all_to_all(
            miss_ids.reshape(device_count, slot_count), BOTH, split_axis=0, concat_axis=0, tiled=True
        ).reshape(-1)
        from_home = features[jnp.minimum(requests, home_rows - 1)]
        blocks = everyones.reshape(-1, block, width_in)
        new_cache = jnp.concatenate(
            [lax.dynamic_index_in_dim(blocks, plan[0, j], 0, keepdims=False) for j in range(CSLOT)], 0
        )
        row = lax.broadcasted_iota(jnp.int32, (cache_rows, requests.shape[0]), 0)
        in_cache = ((requests - home_rows)[None, :] == row).astype(bf16)
        from_cache = contract(in_cache, new_cache, 0, 0).astype(bf16)
        row_data = jnp.where((requests < home_rows)[:, None], from_home, from_cache)
    fetched = lax.all_to_all(
        row_data.reshape(device_count, slot_count, width_in), BOTH, split_axis=0, concat_axis=0, tiled=True
    ).reshape(device_count * slot_count, width_in)

    valid = (
        lax.broadcasted_iota(jnp.int32, (device_count, slot_count), 1)
        < miss_counts.reshape(device_count)[:, None]
    ).reshape(-1)
    hop_used = lax.broadcasted_iota(jnp.int32, (fan2, nodes), 0) < hop_counts[None, :]
    pick_nbr = pick_matrix(nbr_ids.T, hop_used, valid)
    pick_self = pick_matrix(self_ids[None, :], jnp.ones((1, nodes), bool), valid)
    pick_nbr, pick_self = lax.optimization_barrier((pick_nbr.T, pick_self.T))
    hop_div = hop_counts.astype(f32)[:, None]
    seed_div = seed_counts.astype(f32)[:, None]

    used_two = (jnp.arange(fan1, dtype=jnp.int32)[None, :] < seed_counts[:, None]).astype(f32)
    back_self = contract(cotangent, w_self2, 1, 1)
    back_mean = contract(cotangent, w_nbr2, 1, 1) / seed_div
    back_hop = (back_mean[:, None, :] * used_two[:, :, None]).reshape(seeds * fan1, hidden)
    back_hidden = jnp.concatenate([back_self, back_hop], 0)

    own_rows = contract(pick_self, fetched, 1, 0).astype(bf16)
    mean_one = (contract(pick_nbr, fetched, 1, 0) / hop_div).astype(bf16)
    pre = jnp.dot(own_rows, w_self1, preferred_element_type=f32) + jnp.dot(
        mean_one, w_nbr1, preferred_element_type=f32
    )
    gate = jax.nn.sigmoid(pre)
    hidden_one = (pre * gate).astype(bf16)
    back_pre = (back_hidden * gate * (1.0 + pre * (1.0 - gate))).astype(bf16)

    place = lax.broadcasted_iota(jnp.int32, (seeds, nodes), 1) - seeds
    first = lax.broadcasted_iota(jnp.int32, (seeds, nodes), 0) * fan1
    pick_two = ((place >= first) & (place < first + seed_counts[:, None])).astype(bf16)
    seed_rows = hidden_one[:seeds]
    mean_two = (jnp.dot(pick_two, hidden_one, preferred_element_type=f32) / seed_div).astype(bf16)
    embedding = (
        jnp.dot(seed_rows, w_self2, preferred_element_type=f32)
        + jnp.dot(mean_two, w_nbr2, preferred_element_type=f32)
    ).astype(bf16)

    terms_own = contract(back_pre, own_rows, 0, 0).astype(bf16)
    terms_nbr = contract(back_pre, mean_one, 0, 0).astype(bf16)
    rows_two = jnp.concatenate([seed_rows, mean_two], 1)
    if n_dev == 8:
        sum_own, sum_nbr, sum_two = sum_over_devices(n_hst, terms_own, terms_nbr, rows_two, cot_cols.T)
    else:
        terms = jnp.concatenate([terms_own, terms_nbr], 1).reshape(n_hst, n_dev, part, 2 * width_in)
        terms = lax.all_to_all(terms, "dev", split_axis=1, concat_axis=1, tiled=True)
        sum_one = jnp.sum(terms.astype(f32), 1).astype(bf16)
        rows_all = lax.all_gather(rows_two, "dev", axis=0, tiled=True)
        sum_two = contract(cot_cols, rows_all, 0, 0).astype(bf16).reshape(n_hst, part, 2 * hidden)
        both = lax.all_to_all(
            jnp.concatenate([sum_one, sum_two], 2), "hst", split_axis=0, concat_axis=0, tiled=True
        )
        total = jnp.sum(both.astype(f32), 0)
        sum_own, sum_nbr = total[:, :width_in], total[:, width_in : 2 * width_in]
        sum_two = total[:, 2 * width_in :]
    grads = (sum_own.T, sum_nbr.T, sum_two[:, :hidden].T, sum_two[:, hidden:].T)
    return (embedding, new_cache[None], *grads)


def solution(mesh):
    return jax.shard_map(
        local,
        mesh=mesh,
        in_specs=(
            P(BOTH, None),
            P("hst", "dev", None),
            P("hst", "dev"),
            P(BOTH, None, None, None),
            P(BOTH, None, None),
            P(BOTH),
            P(BOTH, None),
            P(BOTH),
            P(BOTH),
            P(),
            P(),
            P(),
            P(),
            P(BOTH, None),
        ),
        out_specs=(
            P(BOTH, None),
            P("hst", "dev", None),
            P(None, BOTH),
            P(None, BOTH),
            P(None, BOTH),
            P(None, BOTH),
        ),
        check_vma=False,
    )
```

```python
import functools

import jax
import jax.numpy as jnp
from jax import lax
from jax.experimental import pallas as pl
from jax.experimental.pallas import tpu as pltpu
from jax.sharding import PartitionSpec as P

CSLOT = 2
BOTH = ("hst", "dev")


def pick_matrix(ids, used, valid, dtype=jnp.bfloat16):
    slots = valid.shape[0]
    slot = lax.broadcasted_iota(jnp.int32, (slots, ids.shape[1]), 0)
    named = jnp.where(used, ids, -1)
    total = jnp.zeros(slot.shape, jnp.float32)
    for k in range(ids.shape[0]):
        total = total + jnp.where(named[k][None, :] == slot, 1.0, 0.0)
    return jnp.where(valid[:, None], total, 0.0).astype(dtype)


def contract(left, right, dim_left, dim_right):
    return lax.dot_general(
        left, right, (((dim_left,), (dim_right,)), ((), ())), preferred_element_type=jnp.float32
    )


def plus(a, b):
    return a.astype(jnp.float32) + b.astype(jnp.float32)


def sum_kernel(n_hst, own_ref, nbr_ref, rows_ref, cot_ref, out_own, out_nbr, out_two,
               own_c, nbr_c, own_1, nbr_1, own_x, nbr_y, own_2, nbr_2, own_y, nbr_x, own_s, nbr_s,
               rows_all, two_s, own_z, nbr_z, two_z, send_sem, recv_sem):
    h, d = lax.axis_index("hst"), lax.axis_index("dev")
    y, x, c = d // 4, (d // 2) % 2, d % 2
    to_core = (h, y * 4 + x * 2 + 1 - c)
    to_x = (h, y * 4 + (1 - x) * 2 + c)
    to_y = (h, (1 - y) * 4 + x * 2 + c)
    to_diag = (h, (1 - y) * 4 + (1 - x) * 2 + c)
    to_hst = [((h + j) % n_hst, d) for j in range(1, n_hst)]
    peers = [to_core, to_x, to_y, to_diag] + to_hst

    barrier = pltpu.get_barrier_semaphore()
    for peer in peers:
        pl.semaphore_signal(barrier, inc=1, device_id=peer, device_id_type=pl.DeviceIdType.MESH)
    pl.semaphore_wait(barrier, len(peers))

    used = [0]

    def send(src, dst, peer):
        k = used[0]
        used[0] = k + 1
        copy = pltpu.make_async_remote_copy(
            src_ref=src, dst_ref=dst, send_sem=send_sem.at[k], recv_sem=recv_sem.at[k],
            device_id=peer, device_id_type=pl.DeviceIdType.MESH,
        )
        copy.start()
        return copy

    own_row = rows_all.at[d]
    rows_x = send(rows_ref, own_row, to_x)
    rows_y = send(rows_ref, own_row, to_y)
    core_own = send(own_ref.at[:, 1 - c], own_c, to_core)
    rows_diag = send(rows_ref, own_row, to_diag)
    core_nbr = send(nbr_ref.at[:, 1 - c], nbr_c, to_core)
    rows_core = [send(rows_ref, own_row, to_core)]
    rows_all[d] = rows_ref[...]

    part = own_ref.shape[2]
    bf16 = own_s.dtype
    count = own_ref.shape[0]

    core_own.wait()

    @pl.loop(0, count)
    def _(i):
        own_1[i // 2, i % 2] = plus(own_ref[i, c], own_c[i]).astype(bf16)

    x_own = send(own_1.at[:, 1 - x], own_x, to_x)
    core_nbr.wait()

    @pl.loop(0, count)
    def _(i):
        nbr_1[i // 4, (i // 2) % 2, i % 2] = plus(nbr_ref[i, c], nbr_c[i]).astype(bf16)

    y_nbr = send(nbr_1.at[:, 1 - y], nbr_y, to_y)

    for copy, peer in ((rows_x, to_x), (rows_y, to_y), (rows_diag, to_diag)):
        copy.wait()
        slot = rows_all.at[peer[1]]
        rows_core.append(send(slot, slot, to_core))
    for copy in rows_core:
        copy.wait()
    wide = rows_all.shape[2]
    gathered = rows_all.shape[0] * rows_all.shape[1]
    tile = 512

    @pl.loop(0, wide // tile)
    def _(t):
        cols = pl.ds(pl.multiple_of(t * tile, tile), tile)
        block = rows_all[:, :, cols].reshape(gathered, tile)
        prod = jnp.dot(cot_ref[...], block, preferred_element_type=jnp.float32)
        two_s[:, :, cols] = prod.astype(bf16).reshape(n_hst, part, tile)

    two_copies = [send(two_s.at[peer[0]], two_z.at[j], peer) for j, peer in enumerate(to_hst)]

    x_own.wait()

    @pl.loop(0, count // 2)
    def _(i):
        own_2[i // 2, i % 2] = plus(own_1[i, x], own_x[i]).astype(bf16)

    y_own = send(own_2.at[:, 1 - y], own_y, to_y)
    y_nbr.wait()

    @pl.loop(0, count // 2)
    def _(i):
        nbr_2[i // 2, i % 2] = plus(nbr_1[i // 2, y, i % 2], nbr_y[i // 2, i % 2]).astype(bf16)

    x_nbr = send(nbr_2.at[:, 1 - x], nbr_x, to_x)

    y_own.wait()

    @pl.loop(0, n_hst)
    def _(i):
        own_s[i] = plus(own_2[i, y], own_y[i]).astype(bf16)

    own_copies = [send(own_s.at[peer[0]], own_z.at[j], peer) for j, peer in enumerate(to_hst)]
    x_nbr.wait()

    @pl.loop(0, n_hst)
    def _(i):
        nbr_s[i] = plus(nbr_2[i, x], nbr_x[i]).astype(bf16)

    nbr_copies = [send(nbr_s.at[peer[0]], nbr_z.at[j], peer) for j, peer in enumerate(to_hst)]

    for copies, mine, landed, out in (
        (two_copies, two_s, two_z, out_two),
        (own_copies, own_s, own_z, out_own),
        (nbr_copies, nbr_s, nbr_z, out_nbr),
    ):
        for copy in copies:
            copy.wait()
        total = mine[h].astype(jnp.float32)
        for j in range(n_hst - 1):
            total = total + landed[j].astype(jnp.float32)
        out[...] = total


def sum_over_devices(n_hst, terms_own, terms_nbr, rows, cot_rows):
    hidden, width = terms_own.shape
    seeds, wide = rows.shape
    part = hidden // (n_hst * 8)
    bf16, f32 = jnp.bfloat16, jnp.float32
    count = n_hst * 4
    vmem = lambda *shape: pltpu.VMEM(shape, bf16)
    others = n_hst - 1
    copies = 13 + 3 * others
    return pl.pallas_call(
        functools.partial(sum_kernel, n_hst),
        out_shape=(
            jax.ShapeDtypeStruct((part, width), f32),
            jax.ShapeDtypeStruct((part, width), f32),
            jax.ShapeDtypeStruct((part, wide), f32),
        ),
        in_specs=[pl.BlockSpec(memory_space=pltpu.VMEM)] * 4,
        out_specs=[pl.BlockSpec(memory_space=pltpu.VMEM)] * 3,
        scratch_shapes=[
            vmem(count, part, width),
            vmem(count, part, width),
            vmem(count // 2, 2, part, width),
            vmem(n_hst, 2, 2, part, width),
            vmem(count // 2, part, width),
            vmem(n_hst, 2, part, width),
            vmem(n_hst, 2, part, width),
            vmem(n_hst, 2, part, width),
            vmem(n_hst, part, width),
            vmem(n_hst, part, width),
            vmem(n_hst, part, width),
            vmem(n_hst, part, width),
            vmem(8, seeds, wide),
            vmem(n_hst, part, wide),
            vmem(others, part, width),
            vmem(others, part, width),
            vmem(others, part, wide),
            pltpu.SemaphoreType.DMA((copies,)),
            pltpu.SemaphoreType.DMA((copies,)),
        ],
        compiler_params=pltpu.CompilerParams(
            collective_id=0, has_side_effects=True, vmem_limit_bytes=40 * 1024 * 1024
        ),
        cost_estimate=pl.CostEstimate(flops=2 * n_hst * part * 8 * seeds * wide, bytes_accessed=2 * hidden * width * 4, transcendentals=0),
        name="sum_over_devices",
    )(
        terms_own.reshape(count, 2, part, width),
        terms_nbr.reshape(count, 2, part, width),
        rows,
        cot_rows,
    )


def serve_kernel(n_hst, plan_ref, cache_ref, home_hbm, ask_ref, cot_ref, new_ref, rows_ref, cots_ref,
                 blocks, home_ref, asked_ref, home_sem, send_sem, recv_sem):
    home_copy = pltpu.make_async_copy(home_hbm, home_ref, home_sem)
    home_copy.start()
    h, d = lax.axis_index("hst"), lax.axis_index("dev")
    y, x, c = d // 4, (d // 2) % 2, d % 2
    place = lambda a, b, e: a * 4 + b * 2 + e
    to_core, to_x, to_y = place(y, x, 1 - c), place(y, 1 - x, c), place(1 - y, x, c)
    to_diag = place(1 - y, 1 - x, c)
    peers = [(d + j) % 8 for j in range(1, 8)]
    me = h * 8 + d
    everyone = [(me + j) % (n_hst * 8) for j in range(1, n_hst * 8)]

    barrier = pltpu.get_barrier_semaphore()
    for q in everyone:
        pl.semaphore_signal(
            barrier, inc=1, device_id=(q // 8, q % 8), device_id_type=pl.DeviceIdType.MESH
        )
    pl.semaphore_wait(barrier, len(everyone))

    used = [0]

    def send(src, dst, peer, plane=h):
        k = used[0]
        used[0] = k + 1
        copy = pltpu.make_async_remote_copy(
            src_ref=src, dst_ref=dst, send_sem=send_sem.at[k], recv_sem=recv_sem.at[k],
            device_id=(plane, peer), device_id_type=pl.DeviceIdType.MESH,
        )
        copy.start()
        return copy

    def pass_on(owner, j, peer):
        slot = blocks.at[owner * CSLOT + j]
        return send(slot, slot, peer)

    own = lambda j, peer: send(cache_ref.at[j], blocks.at[d * CSLOT + j], peer)
    asks = [send(ask_ref.at[q], asked_ref.at[me], q % 8, q // 8) for q in everyone]
    x_first, y_last = own(0, to_x), own(1, to_y)
    x_last, y_first = own(1, to_x), own(0, to_y)
    core = [own(0, to_core), own(1, to_core)]
    cots = [send(cot_ref.at[peer], cots_ref.at[d], peer) for peer in peers]
    for j in range(CSLOT):
        blocks[d * CSLOT + j] = cache_ref[j]
    cots_ref[d] = cot_ref[d]
    asked_ref[me] = ask_ref[me]

    home_rows = home_ref.shape[0]
    slots = ask_ref.shape[2]
    together = 4
    tile = together * slots
    tiles = asked_ref.shape[0] // together
    bf16 = rows_ref.dtype
    diagonal = lax.broadcasted_iota(jnp.int32, (slots, slots), 0) == lax.broadcasted_iota(
        jnp.int32, (slots, slots), 1
    )

    def column(p):
        row = jnp.broadcast_to(asked_ref[p].astype(jnp.float32), (slots, slots))
        return jnp.sum(jnp.where(diagonal, row, 0.0), axis=1, keepdims=True)

    def one_hot(t, first, count):
        asked = jnp.concatenate([column(t * together + u) for u in range(together)], 0)
        at = lax.broadcasted_iota(jnp.int32, (tile, count), 1) + first
        return jnp.where(asked == at.astype(jnp.float32), 1.0, 0.0).astype(bf16)

    home_copy.wait()
    for copy in asks:
        copy.wait()

    def from_home(t):
        rows = pl.ds(pl.multiple_of(t * tile, tile), tile)
        picked = jnp.dot(one_hot(t, 0, home_rows), home_ref[...], preferred_element_type=jnp.float32)
        rows_ref[rows, :] = picked.astype(bf16)

    early, half = tiles // 4, tiles // 2
    pl.loop(0, early)(from_home)

    x_first.wait()
    diag_first = pass_on(to_x, 0, to_y)
    y_last.wait()
    diag_last = pass_on(to_y, 1, to_x)
    core += [pass_on(to_x, 0, to_core), pass_on(to_y, 1, to_core)]

    pl.loop(early, half)(from_home)

    x_last.wait()
    core.append(pass_on(to_x, 1, to_core))
    y_first.wait()
    core.append(pass_on(to_y, 0, to_core))

    pl.loop(half, tiles)(from_home)

    diag_first.wait()
    core.append(pass_on(to_diag, 0, to_core))
    diag_last.wait()
    core.append(pass_on(to_diag, 1, to_core))
    for copy in core + cots:
        copy.wait()

    block = cache_ref.shape[1]
    for j in range(CSLOT):
        new_ref[pl.ds(j * block, block), :] = blocks[plan_ref[0, j]]

    @pl.loop(0, tiles)
    def _(t):
        rows = pl.ds(pl.multiple_of(t * tile, tile), tile)
        hot = one_hot(t, home_rows, CSLOT * block)
        picked = jnp.dot(hot, new_ref[...], preferred_element_type=jnp.float32)
        rows_ref[rows, :] = (rows_ref[rows, :].astype(jnp.float32) + picked).astype(bf16)


def serve_rows(n_hst, plan, cache, home, ask, cot_parts):
    _, block, width = cache.shape
    bf16 = jnp.bfloat16
    asks = ask.shape[0] * ask.shape[2]
    vmem = pl.BlockSpec(memory_space=pltpu.VMEM)
    copies = 20 + ask.shape[0]
    return pl.pallas_call(
        functools.partial(serve_kernel, n_hst),
        out_shape=(
            jax.ShapeDtypeStruct((CSLOT * block, width), bf16),
            jax.ShapeDtypeStruct((asks, width), bf16),
            jax.ShapeDtypeStruct(cot_parts.shape, bf16),
        ),
        in_specs=[pl.BlockSpec(memory_space=pltpu.SMEM), vmem, pl.BlockSpec(memory_space=pl.ANY), vmem, vmem],
        out_specs=[vmem] * 3,
        scratch_shapes=[
            pltpu.VMEM((8 * CSLOT, block, width), bf16),
            pltpu.VMEM(home.shape, bf16),
            pltpu.VMEM(ask.shape, jnp.int32),
            pltpu.SemaphoreType.DMA,
            pltpu.SemaphoreType.DMA((copies,)),
            pltpu.SemaphoreType.DMA((copies,)),
        ],
        compiler_params=pltpu.CompilerParams(
            collective_id=1, has_side_effects=True, vmem_limit_bytes=40 * 1024 * 1024
        ),
        cost_estimate=pl.CostEstimate(
            flops=2 * asks * (home.shape[0] + CSLOT * block) * width,
            bytes_accessed=4 * (asks + home.shape[0]) * width,
            transcendentals=0,
        ),
        name="serve_rows",
    )(plan, cache, home, ask, cot_parts)


def local(
    features,
    cache_blocks,
    plan,
    miss_ids,
    miss_counts,
    self_ids,
    nbr_ids,
    hop_counts,
    seed_counts,
    w_self1,
    w_nbr1,
    w_self2,
    w_nbr2,
    cotangent,
):
    bf16, f32 = jnp.bfloat16, jnp.float32
    home_rows, width_in = features.shape
    slot_count = miss_ids.shape[3]
    n_hst, n_dev = lax.axis_size("hst"), lax.axis_size("dev")
    device_count = n_hst * n_dev
    nodes, fan2 = nbr_ids.shape
    seeds = seed_counts.shape[0]
    fan1 = (nodes - seeds) // seeds
    hidden = w_self1.shape[1]
    part = hidden // device_count
    cache_rows = cache_blocks.shape[1]
    block = cache_rows // CSLOT

    cot_parts = cotangent.reshape(seeds, n_hst, n_dev, part).transpose(2, 0, 1, 3)
    cot_parts = cot_parts.reshape(n_dev, seeds, n_hst * part)
    if n_dev == 8:
        new_cache, row_data, cot_cols = serve_rows(
            n_hst,
            plan,
            cache_blocks.reshape(CSLOT, block, width_in),
            features,
            miss_ids.reshape(device_count, 1, slot_count),
            cot_parts,
        )
        cot_cols = cot_cols.reshape(n_dev * seeds, n_hst * part)
    else:
        everyones = lax.all_gather(cache_blocks[0], "dev", axis=0, tiled=True)
        cot_cols = lax.all_to_all(
            cot_parts, "dev", split_axis=0, concat_axis=0, tiled=True
        ).reshape(n_dev * seeds, n_hst * part)
        requests = lax.all_to_all(
            miss_ids.reshape(device_count, slot_count), BOTH, split_axis=0, concat_axis=0, tiled=True
        ).reshape(-1)
        from_home = features[jnp.minimum(requests, home_rows - 1)]
        blocks = everyones.reshape(-1, block, width_in)
        new_cache = jnp.concatenate(
            [lax.dynamic_index_in_dim(blocks, plan[0, j], 0, keepdims=False) for j in range(CSLOT)], 0
        )
        row = lax.broadcasted_iota(jnp.int32, (cache_rows, requests.shape[0]), 0)
        in_cache = ((requests - home_rows)[None, :] == row).astype(bf16)
        from_cache = contract(in_cache, new_cache, 0, 0).astype(bf16)
        row_data = jnp.where((requests < home_rows)[:, None], from_home, from_cache)
    fetched = lax.all_to_all(
        row_data.reshape(device_count, slot_count, width_in), BOTH, split_axis=0, concat_axis=0, tiled=True
    ).reshape(device_count * slot_count, width_in)

    valid = (
        lax.broadcasted_iota(jnp.int32, (device_count, slot_count), 1)
        < miss_counts.reshape(device_count)[:, None]
    ).reshape(-1)
    hop_used = lax.broadcasted_iota(jnp.int32, (fan2, nodes), 0) < hop_counts[None, :]
    pick_nbr = pick_matrix(nbr_ids.T, hop_used, valid)
    pick_self = pick_matrix(self_ids[None, :], jnp.ones((1, nodes), bool), valid)
    pick_nbr, pick_self = lax.optimization_barrier((pick_nbr.T, pick_self.T))
    hop_div = hop_counts.astype(f32)[:, None]
    seed_div = seed_counts.astype(f32)[:, None]

    used_two = (jnp.arange(fan1, dtype=jnp.int32)[None, :] < seed_counts[:, None]).astype(f32)
    back_self = contract(cotangent, w_self2, 1, 1)
    back_mean = contract(cotangent, w_nbr2, 1, 1) / seed_div
    back_hop = (back_mean[:, None, :] * used_two[:, :, None]).reshape(seeds * fan1, hidden)
    back_hidden = jnp.concatenate([back_self, back_hop], 0)

    own_rows = contract(pick_self, fetched, 1, 0).astype(bf16)
    mean_one = (contract(pick_nbr, fetched, 1, 0) / hop_div).astype(bf16)
    pre = jnp.dot(own_rows, w_self1, preferred_element_type=f32) + jnp.dot(
        mean_one, w_nbr1, preferred_element_type=f32
    )
    gate = jax.nn.sigmoid(pre)
    hidden_one = (pre * gate).astype(bf16)
    back_pre = (back_hidden * gate * (1.0 + pre * (1.0 - gate))).astype(bf16)

    place = lax.broadcasted_iota(jnp.int32, (seeds, nodes), 1) - seeds
    first = lax.broadcasted_iota(jnp.int32, (seeds, nodes), 0) * fan1
    pick_two = ((place >= first) & (place < first + seed_counts[:, None])).astype(bf16)
    seed_rows = hidden_one[:seeds]
    mean_two = (jnp.dot(pick_two, hidden_one, preferred_element_type=f32) / seed_div).astype(bf16)
    embedding = (
        jnp.dot(seed_rows, w_self2, preferred_element_type=f32)
        + jnp.dot(mean_two, w_nbr2, preferred_element_type=f32)
    ).astype(bf16)

    terms_own = contract(back_pre, own_rows, 0, 0).astype(bf16)
    terms_nbr = contract(back_pre, mean_one, 0, 0).astype(bf16)
    rows_two = jnp.concatenate([seed_rows, mean_two], 1)
    if n_dev == 8:
        sum_own, sum_nbr, sum_two = sum_over_devices(n_hst, terms_own, terms_nbr, rows_two, cot_cols.T)
    else:
        terms = jnp.concatenate([terms_own, terms_nbr], 1).reshape(n_hst, n_dev, part, 2 * width_in)
        terms = lax.all_to_all(terms, "dev", split_axis=1, concat_axis=1, tiled=True)
        sum_one = jnp.sum(terms.astype(f32), 1).astype(bf16)
        rows_all = lax.all_gather(rows_two, "dev", axis=0, tiled=True)
        sum_two = contract(cot_cols, rows_all, 0, 0).astype(bf16).reshape(n_hst, part, 2 * hidden)
        both = lax.all_to_all(
            jnp.concatenate([sum_one, sum_two], 2), "hst", split_axis=0, concat_axis=0, tiled=True
        )
        total = jnp.sum(both.astype(f32), 0)
        sum_own, sum_nbr = total[:, :width_in], total[:, width_in : 2 * width_in]
        sum_two = total[:, 2 * width_in :]
    grads = (sum_own.T, sum_nbr.T, sum_two[:, :hidden].T, sum_two[:, hidden:].T)
    return (embedding, new_cache[None], *grads)


def solution(mesh):
    return jax.shard_map(
        local,
        mesh=mesh,
        in_specs=(
            P(BOTH, None),
            P("hst", "dev", None),
            P("hst", "dev"),
            P(BOTH, None, None, None),
            P(BOTH, None, None),
            P(BOTH),
            P(BOTH, None),
            P(BOTH),
            P(BOTH),
            P(),
            P(),
            P(),
            P(),
            P(BOTH, None),
        ),
        out_specs=(
            P(BOTH, None),
            P("hst", "dev", None),
            P(None, BOTH),
            P(None, BOTH),
            P(None, BOTH),
            P(None, BOTH),
        ),
        check_vma=False,
    )
```
